32 devices in a mesh: grp: 2 (over y), gx: 8 (over z, x), gy: 2 (over core).
Axes of the slice: x: 2, y: 2, z: 4, core: 2. Of those that a mesh axis runs over, the one named last changes fastest.
Arguments:
- block: float32 [64, 8, 96, 256], P(None, None, ('grp', 'gx'), 'gy'), parts along dimension 2, may hold values from -6 to 6
- hop: float32 [98, 8, 8], P('grp'), parts along dimension 0, may hold values from -0.3125 to 0.3125
- onsite: float32 [8, 96, 256], P(None, ('grp', 'gx'), 'gy'), parts along dimension 1, may hold values from -1 to 1
- offsets: int32 [49, 2], replicated, may hold values from -3 to 3, as said below
Outputs:
- basis: float32 [64, 8, 96, 256], P(None, None, ('grp', 'gx'), 'gy'), parts along dimension 2
The draws below stay inside these ranges and needn't reach their ends.
There are 2 independent parts, one for each index of `grp`. The reference program is written for one: setup_inputs(seed, part) draws one part's arguments, and reference() takes and returns one part's arrays. A program takes and returns all parts, laid end to end along the dimension named above; an argument that names none is the same for every part. Nothing has to cross between parts.
Inputs may be any that keep to these rules, and one draw needn't show every extreme that they name: `offsets`: each pair (dx, dy) with both entries in -3 .. 3 stands in exactly one row.
All inputs are finite; a program needn't handle non-finite values.
Results may differ from the reference program's by a relative error of at most 0.0001.
Values sent between devices are 32-bit elements; how exact they have to be, the bound alone decides.
A program may use at most 64 MiB of HBM per device.

```python
import jax
import jax.numpy as jnp
from jax import lax

NVEC = 64
ORB = 8
REACH = 3
DEGREE = 4
NB = 49
NX = 48
NY = 256


def draw_offsets(key, part):
    key = jax.random.fold_in(key, 1)
    side = 2 * REACH + 1
    order = jax.random.permutation(key, NB).astype(jnp.int32)
    return jnp.stack([order // side - REACH, order % side - REACH], axis=1).astype(jnp.int32)


def level_of(rng, extent, cuts, smallest, top_value):
    def one(dim, shards_of):
        heights = jax.random.uniform(jax.random.fold_in(jax.random.fold_in(rng, 6), dim), (shards_of,), jnp.float32, smallest / len(cuts), top_value / len(cuts))
        return jnp.repeat(jnp.exp(heights), extent[dim] // shards_of).reshape((-1,) + (1,) * (len(extent) - dim - 1))

    gain = one(*cuts[0])
    for cut in cuts[1:]:
        gain = gain * one(*cut)
    return gain


def normal_values(own_key, extent, spread, bound, cuts=(), held_as=jnp.bfloat16):
    drawn = spread * jax.random.normal(own_key, extent, jnp.float32)
    if cuts:
        drawn = drawn * level_of(own_key, extent, cuts, -0.22, 0.18)
    return jnp.clip(drawn, -bound, bound).astype(held_as)


def setup_inputs(seed: int = 0, part: int = 0) -> dict:
    key_list = jax.random.split(jax.random.key(seed), 5)
    part_splits = jax.random.split(jax.random.fold_in(key_list[4], part), 5)
    block = normal_values(part_splits[0], (NVEC, ORB, NX, NY), 1.0, 6.0, ((2, 8), (3, 2)), jnp.float32)
    hop = normal_values(part_splits[1], (NB, ORB, ORB), (NB * ORB) ** -0.5, 0.3125, (), jnp.float32)
    onsite = jnp.clip(jax.random.uniform(part_splits[2], (ORB, NX, NY), jnp.float32, -1.0, 1.0) * level_of(part_splits[2], (ORB, NX, NY), ((1, 8), (2, 2)), -0.4, 0.0), -1.0, 1.0)
    offsets = draw_offsets(jax.random.fold_in(key_list[4], 71), part)
    return dict(block=block, hop=hop, onsite=onsite, offsets=offsets)


shift_centre = 1.25
half_width = 2.25

def build_stencil(hop, offsets):
    side = 2 * REACH + 1
    position = (offsets[:, 0] + REACH) * side + (offsets[:, 1] + REACH)
    slots = jnp.arange(NB, dtype=jnp.int32)
    onehot = (position[:, None] == slots[None, :]).astype(jnp.float32)
    flat = jnp.dot(onehot.T.astype(jnp.float32), hop.reshape(NB, ORB * ORB).astype(jnp.float32), precision=lax.Precision.HIGHEST, preferred_element_type=jnp.float32)
    raw = jnp.transpose(flat.reshape(side, side, ORB, ORB), (2, 3, 0, 1))
    mirror = jnp.transpose(raw, (1, 0, 2, 3))[:, :, ::-1, ::-1]
    return 0.5 * (raw + mirror)

def hopping(padded, stencil):
    return lax.conv_general_dilated(padded, stencil, (1, 1), 'VALID', dimension_numbers=('NCHW', 'OIHW', 'NCHW'), precision=lax.Precision.HIGHEST, preferred_element_type=jnp.float32)

def reference(block, hop, onsite, offsets):
    stencil = build_stencil(hop, offsets)

    def apply_ham(field):
        padded = jnp.pad(field, ((0, 0), (0, 0), (REACH, REACH), (REACH, REACH)), mode='wrap')
        return hopping(padded, stencil) + onsite[None] * field

    def filter_block(start):
        previous = start
        current = (apply_ham(start) - shift_centre * start) / half_width
        for step in range(DEGREE - 1):
            following = 2.0 * (apply_ham(current) - shift_centre * current) / half_width - previous
            previous, current = (current, following)
        return current
    pieces = block.reshape(NVEC // 8, 8, ORB, NX, NY)
    filtered = lax.map(filter_block, pieces).reshape(NVEC, ORB * NX * NY)
    gram = jnp.dot(filtered.astype(jnp.float32), filtered.T.astype(jnp.float32), precision=lax.Precision.HIGHEST, preferred_element_type=jnp.float32) / (ORB * NX * NY)
    lower = jnp.linalg.cholesky(gram)
    inverse = lax.linalg.triangular_solve(lower, jnp.eye(NVEC, dtype=jnp.float32), left_side=True, lower=True)
    basis = jnp.dot(inverse.astype(jnp.float32), filtered.astype(jnp.float32), precision=lax.Precision.HIGHEST, preferred_element_type=jnp.float32)
    return basis.reshape(NVEC, ORB, NX, NY)
```

```python
import functools

import jax
import jax.numpy as jnp
from jax import lax
from jax.experimental import pallas as pl
from jax.experimental.pallas import tpu as pltpu
from jax.sharding import PartitionSpec as P

ORB = 8
REACH = 3
DEGREE = 4
NB = 49


shift_centre = 1.25
half_width = 2.25


def padded_2(array, sides, width):
    for axis, dim in sides:
        peers, length = (lax.axis_size(axis), array.shape[dim])
        up = [(i, (i + 1) % peers) for i in range(peers)]
        down = [(j, i) for i, j in up]
        last = lax.slice_in_dim(array, length - width, length, axis=dim)
        first = lax.slice_in_dim(array, 0, width, axis=dim)
        before = lax.ppermute(last, axis, up)
        after = lax.ppermute(first, axis, down)
        array = jnp.concatenate([before, array, after], axis=dim)
    return array


def build_stencil(hop, offsets):
    side = 2 * REACH + 1
    position = (offsets[:, 0] + REACH) * side + (offsets[:, 1] + REACH)
    slots = jnp.arange(NB, dtype=jnp.int32)
    onehot = (position[:, None] == slots[None, :]).astype(jnp.float32)
    flat = jnp.dot(
        onehot.T,
        hop.reshape(NB, ORB * ORB),
        precision=lax.Precision.HIGHEST,
        preferred_element_type=jnp.float32,
    )
    raw = jnp.transpose(flat.reshape(side, side, ORB, ORB), (2, 3, 0, 1))
    mirror = jnp.transpose(raw, (1, 0, 2, 3))[:, :, ::-1, ::-1]
    return 0.5 * (raw + mirror)


def hopping(padded, stencil):
    return lax.conv_general_dilated(
        padded,
        stencil,
        (1, 1),
        "VALID",
        dimension_numbers=("NCHW", "OIHW", "NCHW"),
        precision=lax.Precision.HIGHEST,
        preferred_element_type=jnp.float32,
    )


def extend(field, width):
    return padded_2(field, (("gx", 2), ("gy", 3)), width)


def advance(hopped, current, energies, previous):
    return (
        2.0 * (hopped + energies[None] * current - shift_centre * current) / half_width - previous
    )


def per_device_halo(block, hop, onsite, offsets):
    stencil = build_stencil(hop, offsets)
    vectors = block.shape[0]
    first_hop = hopping(extend(block, REACH), stencil)
    current = (first_hop + onsite[None] * block - shift_centre * block) / half_width
    previous = block
    for step in range(DEGREE - 1):
        following = advance(hopping(extend(current, REACH), stencil), current, onsite, previous)
        previous, current = (current, following)
    local_rows = current.shape[1] * current.shape[2] * current.shape[3]
    flat = current.reshape(vectors, local_rows)
    local_gram = jnp.dot(
        flat, flat.T, precision=lax.Precision.HIGHEST, preferred_element_type=jnp.float32
    )
    total_rows = local_rows * lax.axis_size("gx") * lax.axis_size("gy")
    gram = lax.psum(local_gram, ("gx", "gy")) / total_rows
    lower = jnp.linalg.cholesky(gram)
    inverse = lax.linalg.triangular_solve(
        lower, jnp.eye(vectors, dtype=jnp.float32), left_side=True, lower=True
    )
    basis = jnp.dot(
        inverse, flat, precision=lax.Precision.HIGHEST, preferred_element_type=jnp.float32
    )
    return basis.reshape(current.shape)


LANES = 128
TY = 16
MESH = pl.DeviceIdType.MESH


def split_bf16(value):
    high = value.astype(jnp.bfloat16)
    low = (value - high.astype(jnp.float32)).astype(jnp.bfloat16)
    return high, low


def band_weights(stencil):
    side = 2 * REACH + 1
    t = jnp.transpose(stencil, (2, 3, 1, 0)).reshape(side * side * ORB, ORB)
    lane = jnp.arange(LANES)
    spread = (lane[None, :] // TY == jnp.arange(ORB)[:, None]).astype(jnp.float32)
    wide = jnp.dot(t, spread, precision=lax.Precision.HIGHEST, preferred_element_type=jnp.float32)
    wide = wide.reshape(side, side, 1, ORB, 1, LANES)
    yy = jnp.arange(TY)
    rel = jnp.stack([yy, jnp.where(yy < TY // 2, yy + TY, yy - TY)])
    dy = rel[:, :, None] - (lane % TY)[None, None, :]
    total = jnp.zeros((side, 2, ORB, TY, LANES), jnp.float32)
    for k in range(side):
        total = total + jnp.where((dy == k - REACH)[None, :, None], wide[:, k], 0.0)
    band = total.reshape(side, 2 * LANES, LANES)
    zero = jnp.zeros((1, 2 * LANES, LANES), jnp.float32)
    full = jnp.concatenate(
        [jnp.concatenate([band, zero], axis=0), jnp.concatenate([zero, band], axis=0)], axis=2
    )
    high = lax.reduce_precision(full, 8, 7)
    return high.astype(jnp.bfloat16), (full - high).astype(jnp.bfloat16)


def swap_blocks(value):
    row = lax.broadcasted_iota(jnp.int32, value.shape, 1)
    blk = lax.broadcasted_iota(jnp.int32, value.shape, 2) // TY
    for bit in (1, 2, 4):
        a = (row // bit) % 2
        b = (blk // bit) % 2
        up = pltpu.roll(pltpu.roll(value, 8 - bit, 1), TY * bit, 2)
        down = up if bit == 4 else pltpu.roll(pltpu.roll(value, bit, 1), LANES - TY * bit, 2)
        value = jnp.where(a == b, value, jnp.where(a < b, up, down))
    return value


def filter_kernel(
    sizes, block_ref, onsite_ref, wh_ref, wl_ref, out_ref, gram_ref,
    recv, energies, state, sh, sl, back, gathered, grams,
    send_sems, recv_sems, local_sems, back_send, back_recv, back_local, gram_send, gram_recv,
):
    ngx, ngy, chunks, lx = sizes
    peers = ngx * ngy
    nx = ngx * lx
    half = nx // 2
    piece = lx * ORB
    gx, gy = lax.axis_index("gx"), lax.axis_index("gy")
    me = gx * ngy + gy

    def peer(k):
        other = lax.rem(me + k, peers)
        return other, {"gx": other // ngy, "gy": lax.rem(other, ngy)}

    barrier = pltpu.get_barrier_semaphore()

    def greet(k, carry):
        pl.semaphore_signal(barrier, inc=1, device_id=peer(k)[1], device_id_type=MESH)
        return carry

    lax.fori_loop(1, peers, greet, 0)
    pl.semaphore_wait(barrier, peers - 1)

    def rows_of(vector):
        return pl.ds(vector * piece, piece)

    def landing(c):
        return recv.at[c, gy, pl.ds(gx * piece, piece)]

    def send_onsite(k, carry):
        pltpu.make_async_remote_copy(
            src_ref=onsite_ref, dst_ref=landing(chunks), send_sem=send_sems.at[chunks],
            recv_sem=recv_sems.at[chunks], device_id=peer(k)[1], device_id_type=MESH,
        ).start()
        return carry

    pltpu.make_async_copy(onsite_ref, landing(chunks), local_sems.at[chunks]).start()
    lax.fori_loop(1, peers, send_onsite, 0)

    def send_chunk(c, carry):
        pltpu.make_async_copy(
            block_ref.at[rows_of(c * peers + me)], landing(c), local_sems.at[c]
        ).start()

        def one(k, carry):
            other, where = peer(k)
            pltpu.make_async_remote_copy(
                src_ref=block_ref.at[rows_of(c * peers + other)], dst_ref=landing(c),
                send_sem=send_sems.at[c], recv_sem=recv_sems.at[c],
                device_id=where, device_id_type=MESH,
            ).start()
            return carry

        return lax.fori_loop(1, peers, one, carry)

    lax.fori_loop(0, chunks, send_chunk, 0)

    others = (peers - 1) * piece

    def wait_chunk(c):
        pltpu.make_async_copy(
            block_ref.at[pl.ds(0, others)], gathered.at[pl.ds(0, others)], recv_sems.at[c]
        ).wait()
        pltpu.make_async_copy(block_ref.at[pl.ds(0, piece)], landing(c), local_sems.at[c]).wait()

    def unpack(c, store):
        for g in range(ngy):
            for q in range(0, nx, 8):
                tile = recv[c, g, pl.ds(q * ORB, 8 * ORB)].reshape(8, ORB, LANES)
                tile = swap_blocks(tile)
                for i in range(8):
                    x = q + i
                    store(x % 2, x // 2, g, tile[i])

    wait_chunk(chunks)

    def store_energy(xr, r, g, tile):
        energies[xr, r, pl.ds(g * 8, 8), :] = tile - shift_centre

    unpack(chunks, store_energy)

    lane = lax.broadcasted_iota(jnp.int32, (1, TY, LANES), 2)
    near = lax.rem(lane, TY) < TY // 2
    low_rows = {1: (1, [(0, half - 1), (half + 1, 0), (half + 2, 1)]),
                0: (2, [(0, half - 2), (1, half - 1), (half + 2, 0)])}

    def one_chunk(c, carry):
        wait_chunk(c)

        def store_state(xr, r, g, tile):
            state[0, xr, r, pl.ds(g * 8, 8), :] = tile
            state[1, xr, r, pl.ds(g * 8, 8), :] = jnp.zeros_like(tile)

        unpack(c, store_state)

        def step(k, carry):
            now = lax.rem(k, 2)
            for xr in range(2):
                par = 1 - xr
                start, wraps = low_rows[par]
                for r in range(0, half, 4):
                    v = state[now, xr, pl.ds(r, 4)]
                    edge = jnp.where(near, pltpu.roll(v, TY - 1, 1), pltpu.roll(v, 1, 1))
                    both = jnp.concatenate([v, edge], axis=2)
                    high, low = split_bf16(both)
                    sh[par, pl.ds(start + r, 4)] = high
                    sl[par, pl.ds(start + r, 4)] = low
                for to, r in wraps:
                    sh[par, to] = sh[par, start + r]
                    sl[par, to] = sl[par, start + r]
            alpha = jnp.where(k == 0, 1.0 / half_width, 2.0 / half_width)
            for r in range(0, half, 8):
                acc = jnp.zeros((8 * TY, 2 * LANES), jnp.float32)
                for j in range(2 * REACH + 2):
                    rows = pl.ds(r + j // 2, 8)
                    vh = sh[j % 2, rows].reshape(8 * TY, 2 * LANES)
                    vl = sl[j % 2, rows].reshape(8 * TY, 2 * LANES)
                    acc += jnp.dot(vh, wh_ref[j], preferred_element_type=jnp.float32)
                    acc += jnp.dot(vl, wh_ref[j], preferred_element_type=jnp.float32)
                    acc += jnp.dot(vh, wl_ref[j], preferred_element_type=jnp.float32)
                for xr in range(2):
                    hopped = acc[:, xr * LANES:(xr + 1) * LANES].reshape(8, TY, LANES)
                    v = state[now, xr, pl.ds(r, 8)]
                    e = energies[xr, pl.ds(r, 8)]
                    old = state[1 - now, xr, pl.ds(r, 8)]
                    state[1 - now, xr, pl.ds(r, 8)] = alpha * (hopped + e * v) - old
            return carry

        lax.fori_loop(0, DEGREE, step, 0)

        for g in range(ngy):
            for q in range(0, nx, 8):
                tile = jnp.stack(
                    [state[DEGREE % 2, (q + i) % 2, (q + i) // 2, pl.ds(g * 8, 8), :] for i in range(8)]
                )
                back[c, g, pl.ds(q * ORB, 8 * ORB)] = swap_blocks(tile).reshape(8 * ORB, LANES)

        home = rows_of(c * peers + me)
        pltpu.make_async_copy(
            back.at[c, gy, pl.ds(gx * piece, piece)], gathered.at[home], back_local.at[c]
        ).start()

        def one(k, carry):
            other, where = peer(k)
            pltpu.make_async_remote_copy(
                src_ref=back.at[c, lax.rem(other, ngy), pl.ds((other // ngy) * piece, piece)],
                dst_ref=gathered.at[home], send_sem=back_send.at[c], recv_sem=back_recv.at[c],
                device_id=where, device_id_type=MESH,
            ).start()
            return carry

        return lax.fori_loop(1, peers, one, carry)

    lax.fori_loop(0, chunks, one_chunk, 0)

    def wait_back(c, carry):
        pltpu.make_async_copy(
            block_ref.at[pl.ds(0, others)], gathered.at[pl.ds(0, others)], back_recv.at[c]
        ).wait()
        pltpu.make_async_copy(
            block_ref.at[pl.ds(0, piece)], gathered.at[pl.ds(0, piece)], back_local.at[c]
        ).wait()
        return carry

    lax.fori_loop(0, chunks, wait_back, 0)

    nvec = chunks * peers
    total = jnp.zeros((2 * nvec, nvec), jnp.float32)

    def gram_step(q, total):
        a = gathered[pl.ds(2 * q, nvec, stride=piece), :]
        b = gathered[pl.ds(2 * q + 1, nvec, stride=piece), :]
        high, low = split_bf16(jnp.concatenate([a, b], axis=1))
        return total + lax.dot_general(
            jnp.concatenate([high, low], axis=0), high, (((1,), (1,)), ((), ())),
            preferred_element_type=jnp.float32,
        )

    total = lax.fori_loop(0, piece // 2, gram_step, total)
    cross = total[nvec:]
    local = total[:nvec] + cross + cross.T
    grams[me] = jnp.concatenate([local[: nvec // 2], local[nvec // 2:]], axis=1)

    def send_gram(k, carry):
        pltpu.make_async_remote_copy(
            src_ref=grams.at[me], dst_ref=grams.at[me], send_sem=gram_send,
            recv_sem=gram_recv, device_id=peer(k)[1], device_id_type=MESH,
        ).start()
        return carry

    lax.fori_loop(1, peers, send_gram, 0)
    out_copy = pltpu.make_async_copy(gathered, out_ref, local_sems.at[chunks])
    out_copy.start()
    pltpu.make_async_copy(
        grams.at[pl.ds(0, peers - 1)], grams.at[pl.ds(0, peers - 1)], gram_recv
    ).wait()
    total = grams[0]
    for d in range(1, peers):
        total = total + grams[d]
    gram_ref[...] = total

    def drain(c, carry):
        pltpu.make_async_copy(
            block_ref.at[pl.ds(0, others)], gathered.at[pl.ds(0, others)], send_sems.at[c]
        ).wait()
        return carry

    lax.fori_loop(0, chunks + 1, drain, 0)

    def drain_back(c, carry):
        pltpu.make_async_copy(
            block_ref.at[pl.ds(0, others)], gathered.at[pl.ds(0, others)], back_send.at[c]
        ).wait()
        return carry

    lax.fori_loop(0, chunks, drain_back, 0)
    pltpu.make_async_copy(
        grams.at[pl.ds(0, peers - 1)], grams.at[pl.ds(0, peers - 1)], gram_send
    ).wait()
    out_copy.wait()


def per_device_whole(block, hop, onsite, offsets):
    ngx, ngy = lax.axis_size("gx"), lax.axis_size("gy")
    peers = ngx * ngy
    nvec, _, lx, ly = block.shape
    chunks = nvec // peers
    nx = ngx * lx
    piece = lx * ORB
    wh, wl = band_weights(build_stencil(hop, offsets))
    rows = jnp.transpose(block, (0, 2, 1, 3)).reshape(nvec * piece, ly)
    energy_rows = jnp.transpose(onsite, (1, 0, 2)).reshape(piece, ly)
    vmem = pl.BlockSpec(memory_space=pltpu.VMEM)
    hbm = pl.BlockSpec(memory_space=pl.ANY)
    filtered, packed = pl.pallas_call(
        functools.partial(filter_kernel, (ngx, ngy, chunks, lx)),
        out_shape=(
            jax.ShapeDtypeStruct((nvec * piece, ly), jnp.float32),
            jax.ShapeDtypeStruct((nvec // 2, LANES), jnp.float32),
        ),
        in_specs=[vmem, vmem, vmem, vmem],
        out_specs=(hbm, vmem),
        scratch_shapes=[
            pltpu.VMEM((chunks + 1, ngy, nx * ORB, LANES), jnp.float32),
            pltpu.VMEM((2, nx // 2, TY, LANES), jnp.float32),
            pltpu.VMEM((2, 2, nx // 2, TY, LANES), jnp.float32),
            pltpu.VMEM((2, nx // 2 + REACH, TY, 2 * LANES), jnp.bfloat16),
            pltpu.VMEM((2, nx // 2 + REACH, TY, 2 * LANES), jnp.bfloat16),
            pltpu.VMEM((chunks, ngy, nx * ORB, LANES), jnp.float32),
            pltpu.VMEM((nvec * piece, LANES), jnp.float32),
            pltpu.VMEM((peers, nvec // 2, LANES), jnp.float32),
            pltpu.SemaphoreType.DMA((chunks + 1,)),
            pltpu.SemaphoreType.DMA((chunks + 1,)),
            pltpu.SemaphoreType.DMA((chunks + 1,)),
            pltpu.SemaphoreType.DMA((chunks,)),
            pltpu.SemaphoreType.DMA((chunks,)),
            pltpu.SemaphoreType.DMA((chunks,)),
            pltpu.SemaphoreType.DMA,
            pltpu.SemaphoreType.DMA,
        ],
        compiler_params=pltpu.CompilerParams(
            collective_id=0, has_side_effects=True, vmem_limit_bytes=48 * 1024 * 1024
        ),
    )(rows, energy_rows, wh, wl)
    gram = jnp.concatenate([packed[:, :nvec], packed[:, nvec:]], axis=0)
    gram = gram / (piece * ly * peers)
    lower = jnp.linalg.cholesky(gram)
    inverse = lax.linalg.triangular_solve(
        lower, jnp.eye(nvec, dtype=jnp.float32), left_side=True, lower=True
    )
    return jnp.einsum(
        "mn,nxoy->moxy", inverse, filtered.reshape(nvec, lx, ORB, ly),
        precision=lax.Precision.HIGHEST, preferred_element_type=jnp.float32,
    )


def per_device(block, hop, onsite, offsets):
    ngx, ngy = lax.axis_size("gx"), lax.axis_size("gy")
    nvec, orbitals, lx, ly = block.shape
    fits = (
        nvec % (ngx * ngy) == 0 and nvec == 64 and orbitals == ORB and ly == LANES
        and ngy == 2 and (ngx * lx) % 16 == 0
    )
    return (per_device_whole if fits else per_device_halo)(block, hop, onsite, offsets)


def solution(mesh):
    return jax.shard_map(
        per_device,
        mesh=mesh,
        in_specs=(
            P(None, None, ("grp", "gx"), "gy"),
            P("grp", None, None),
            P(None, ("grp", "gx"), "gy"),
            P(),
        ),
        out_specs=P(None, None, ("grp", "gx"), "gy"),
        check_vma=False,
    )
```

```python
import functools

import jax
import jax.numpy as jnp
from jax import lax
from jax.experimental import pallas as pl
from jax.experimental.pallas import tpu as pltpu
from jax.sharding import PartitionSpec as P

ORB = 8
REACH = 3
DEGREE = 4
NB = 49


shift_centre = 1.25
half_width = 2.25


def padded_2(array, sides, width):
    for axis, dim in sides:
        peers, length = (lax.axis_size(axis), array.shape[dim])
        up = [(i, (i + 1) % peers) for i in range(peers)]
        down = [(j, i) for i, j in up]
        last = lax.slice_in_dim(array, length - width, length, axis=dim)
        first = lax.slice_in_dim(array, 0, width, axis=dim)
        before = lax.ppermute(last, axis, up)
        after = lax.ppermute(first, axis, down)
        array = jnp.concatenate([before, array, after], axis=dim)
    return array


def build_stencil(hop, offsets):
    side = 2 * REACH + 1
    position = (offsets[:, 0] + REACH) * side + (offsets[:, 1] + REACH)
    slots = jnp.arange(NB, dtype=jnp.int32)
    onehot = (position[:, None] == slots[None, :]).astype(jnp.float32)
    flat = jnp.dot(
        onehot.T,
        hop.reshape(NB, ORB * ORB),
        precision=lax.Precision.HIGHEST,
        preferred_element_type=jnp.float32,
    )
    raw = jnp.transpose(flat.reshape(side, side, ORB, ORB), (2, 3, 0, 1))
    mirror = jnp.transpose(raw, (1, 0, 2, 3))[:, :, ::-1, ::-1]
    return 0.5 * (raw + mirror)


def hopping(padded, stencil):
    return lax.conv_general_dilated(
        padded,
        stencil,
        (1, 1),
        "VALID",
        dimension_numbers=("NCHW", "OIHW", "NCHW"),
        precision=lax.Precision.HIGHEST,
        preferred_element_type=jnp.float32,
    )


def extend(field, width):
    return padded_2(field, (("gx", 2), ("gy", 3)), width)


def advance(hopped, current, energies, previous):
    return (
        2.0 * (hopped + energies[None] * current - shift_centre * current) / half_width - previous
    )


def per_device_halo(block, hop, onsite, offsets):
    stencil = build_stencil(hop, offsets)
    vectors = block.shape[0]
    first_hop = hopping(extend(block, REACH), stencil)
    current = (first_hop + onsite[None] * block - shift_centre * block) / half_width
    previous = block
    for step in range(DEGREE - 1):
        following = advance(hopping(extend(current, REACH), stencil), current, onsite, previous)
        previous, current = (current, following)
    local_rows = current.shape[1] * current.shape[2] * current.shape[3]
    flat = current.reshape(vectors, local_rows)
    local_gram = jnp.dot(
        flat, flat.T, precision=lax.Precision.HIGHEST, preferred_element_type=jnp.float32
    )
    total_rows = local_rows * lax.axis_size("gx") * lax.axis_size("gy")
    gram = lax.psum(local_gram, ("gx", "gy")) / total_rows
    lower = jnp.linalg.cholesky(gram)
    inverse = lax.linalg.triangular_solve(
        lower, jnp.eye(vectors, dtype=jnp.float32), left_side=True, lower=True
    )
    basis = jnp.dot(
        inverse, flat, precision=lax.Precision.HIGHEST, preferred_element_type=jnp.float32
    )
    return basis.reshape(current.shape)


LANES = 128
TY = 16
MESH = pl.DeviceIdType.MESH


def split_bf16(value):
    high = value.astype(jnp.bfloat16)
    low = (value - high.astype(jnp.float32)).astype(jnp.bfloat16)
    return high, low


def spread_stencil(stencil):
    side = 2 * REACH + 1
    t = jnp.transpose(stencil, (2, 3, 1, 0)).reshape(side * side * ORB, ORB)
    lane = jnp.arange(LANES)
    spread = (lane[None, :] // TY == jnp.arange(ORB)[:, None]).astype(jnp.float32)
    return jnp.dot(t, spread, precision=lax.Precision.HIGHEST, preferred_element_type=jnp.float32)


def band_weights(wide_ref, wh_ref, wl_ref):
    side = 2 * REACH + 1
    yy = lax.broadcasted_iota(jnp.int32, (TY, LANES), 0)
    y = lax.rem(lax.broadcasted_iota(jnp.int32, (TY, LANES), 1), TY)
    empty = jnp.zeros((2 * LANES, LANES), jnp.bfloat16)
    for ref in (wh_ref, wl_ref):
        ref[0, :, pl.ds(LANES, LANES)] = empty
        ref[side, :, pl.ds(0, LANES)] = empty

    def one(dx, carry):
        for part in range(2):
            rel = yy if part == 0 else jnp.where(yy < TY // 2, yy + TY, yy - TY)
            dy = rel - y
            for p in range(ORB):
                total = jnp.zeros((TY, LANES), jnp.float32)
                for k in range(side):
                    row = wide_ref[dx, k, pl.ds(p, 1), :]
                    total = jnp.where(dy == k - REACH, row, total)
                high, low = split_bf16(total)
                rows = pl.ds(part * LANES + p * TY, TY)
                for xr in range(2):
                    wh_ref[dx + xr, rows, pl.ds(xr * LANES, LANES)] = high
                    wl_ref[dx + xr, rows, pl.ds(xr * LANES, LANES)] = low
        return carry

    lax.fori_loop(0, side, one, 0)


def swap_blocks(value):
    row = lax.broadcasted_iota(jnp.int32, value.shape, 1)
    blk = lax.broadcasted_iota(jnp.int32, value.shape, 2) // TY
    for bit in (1, 2, 4):
        a = (row // bit) % 2
        b = (blk // bit) % 2
        up = pltpu.roll(pltpu.roll(value, 8 - bit, 1), TY * bit, 2)
        down = up if bit == 4 else pltpu.roll(pltpu.roll(value, bit, 1), LANES - TY * bit, 2)
        value = jnp.where(a == b, value, jnp.where(a < b, up, down))
    return value


def filter_kernel(
    sizes, block_ref, onsite_ref, wide_ref, out_ref, gram_ref,
    wh_ref, wl_ref, recv, columns, energies, state, sh, sl, back, gathered, grams, sums,
    send_sems, recv_sems, local_sems, back_send, back_recv, back_local, small_send, small_recv, out_sem,
):
    ngx, ngy, chunks, lx = sizes
    peers = ngx * ngy
    nx = ngx * lx
    half = nx // 2
    piece = lx * ORB
    gx, gy = lax.axis_index("gx"), lax.axis_index("gy")
    me = gx * ngy + gy

    def peer(k):
        other = lax.rem(me + k, peers)
        return other, {"gx": other // ngy, "gy": lax.rem(other, ngy)}

    barrier = pltpu.get_barrier_semaphore()

    def greet(k, carry):
        pl.semaphore_signal(barrier, inc=1, device_id=peer(k)[1], device_id_type=MESH)
        return carry

    lax.fori_loop(1, peers, greet, 0)
    pl.semaphore_wait(barrier, peers - 1)

    def rows_of(vector):
        return pl.ds(vector * piece, piece)

    def landing(c):
        return recv.at[c, gy, pl.ds(gx * piece, piece)]

    plane = 2 * ngy
    nz = ngx // 2
    z, col = gx // 2, lax.rem(gx, 2)
    spot = col * ngy + gy

    def along(k):
        return {"gx": lax.rem(z + k, nz) * 2 + col, "gy": gy}

    def across(k):
        other = lax.rem(spot + k, plane)
        return {"gx": z * 2 + other // ngy, "gy": lax.rem(other, ngy)}

    def share(count, where, ref, sem):
        def one(k, carry):
            pltpu.make_async_remote_copy(
                src_ref=ref, dst_ref=ref, send_sem=small_send.at[sem],
                recv_sem=small_recv.at[sem], device_id=where(k), device_id_type=MESH,
            ).start()
            return carry

        lax.fori_loop(1, count, one, 0)

    def settle(refs, sems, sem):
        pltpu.make_async_copy(refs, refs, sems.at[sem]).wait()

    columns[spot, pl.ds(z * piece, piece)] = onsite_ref[...]
    share(nz, along, columns.at[spot, pl.ds(z * piece, piece)], 0)

    def send_chunk(c, carry):
        pltpu.make_async_copy(
            block_ref.at[rows_of(c * peers + me)], landing(c), local_sems.at[c]
        ).start()

        def one(k, carry):
            other, where = peer(k)
            pltpu.make_async_remote_copy(
                src_ref=block_ref.at[rows_of(c * peers + other)], dst_ref=landing(c),
                send_sem=send_sems.at[c], recv_sem=recv_sems.at[c],
                device_id=where, device_id_type=MESH,
            ).start()
            return carry

        return lax.fori_loop(1, peers, one, carry)

    send_chunk(0, 0)
    settle(columns.at[0, pl.ds(0, (nz - 1) * piece)], small_recv, 0)
    share(plane, across, columns.at[spot], 1)
    lax.fori_loop(1, chunks, send_chunk, 0)
    band_weights(wide_ref, wh_ref, wl_ref)

    others = (peers - 1) * piece

    def wait_chunk(c):
        pltpu.make_async_copy(
            block_ref.at[pl.ds(0, others)], gathered.at[pl.ds(0, others)], recv_sems.at[c]
        ).wait()
        pltpu.make_async_copy(block_ref.at[pl.ds(0, piece)], landing(c), local_sems.at[c]).wait()

    def unpack(c, store):
        for g in range(ngy):
            for q in range(0, nx, 8):
                tile = recv[c, g, pl.ds(q * ORB, 8 * ORB)].reshape(8, ORB, LANES)
                tile = swap_blocks(tile)
                for i in range(8):
                    x = q + i
                    store(x % 2, x // 2, g, tile[i])

    settle(columns.at[pl.ds(0, plane - 1)], small_recv, 1)
    for other in range(plane):
        for q in range(nz):
            tile = columns[other, pl.ds(q * piece, piece)].reshape(lx, ORB, LANES)
            tile = swap_blocks(tile) - shift_centre
            for i in range(lx):
                x = (2 * q + other // ngy) * lx + i
                energies[x % 2, x // 2, pl.ds((other % ngy) * 8, 8), :] = tile[i]

    lane = lax.broadcasted_iota(jnp.int32, (1, TY, LANES), 2)
    near = lax.rem(lane, TY) < TY // 2
    low_rows = {1: (1, [(0, half - 1), (half + 1, 0), (half + 2, 1)]),
                0: (2, [(0, half - 2), (1, half - 1), (half + 2, 0)])}

    def one_chunk(c, carry):
        wait_chunk(c)

        def store_state(xr, r, g, tile):
            state[0, xr, r, pl.ds(g * 8, 8), :] = tile
            state[1, xr, r, pl.ds(g * 8, 8), :] = jnp.zeros_like(tile)

        unpack(c, store_state)

        def step(k, carry):
            now = lax.rem(k, 2)
            for xr in range(2):
                par = 1 - xr
                start, wraps = low_rows[par]
                for r in range(0, half, 4):
                    v = state[now, xr, pl.ds(r, 4)]
                    edge = jnp.where(near, pltpu.roll(v, TY - 1, 1), pltpu.roll(v, 1, 1))
                    both = jnp.concatenate([v, edge], axis=2)
                    high, low = split_bf16(both)
                    sh[par, pl.ds(start + r, 4)] = high
                    sl[par, pl.ds(start + r, 4)] = low
                for to, r in wraps:
                    sh[par, to] = sh[par, start + r]
                    sl[par, to] = sl[par, start + r]
            alpha = jnp.where(k == 0, 1.0 / half_width, 2.0 / half_width)
            for r in range(0, half, 8):
                acc = jnp.zeros((8 * TY, 2 * LANES), jnp.float32)
                for j in range(2 * REACH + 2):
                    rows = pl.ds(r + j // 2, 8)
                    vh = sh[j % 2, rows].reshape(8 * TY, 2 * LANES)
                    vl = sl[j % 2, rows].reshape(8 * TY, 2 * LANES)
                    acc += jnp.dot(vh, wh_ref[j], preferred_element_type=jnp.float32)
                    acc += jnp.dot(vl, wh_ref[j], preferred_element_type=jnp.float32)
                    acc += jnp.dot(vh, wl_ref[j], preferred_element_type=jnp.float32)
                for xr in range(2):
                    hopped = acc[:, xr * LANES:(xr + 1) * LANES].reshape(8, TY, LANES)
                    v = state[now, xr, pl.ds(r, 8)]
                    e = energies[xr, pl.ds(r, 8)]
                    old = state[1 - now, xr, pl.ds(r, 8)]
                    state[1 - now, xr, pl.ds(r, 8)] = alpha * (hopped + e * v) - old
            return carry

        lax.fori_loop(0, DEGREE, step, 0)

        for g in range(ngy):
            for q in range(0, nx, 8):
                tile = jnp.stack(
                    [state[DEGREE % 2, (q + i) % 2, (q + i) // 2, pl.ds(g * 8, 8), :] for i in range(8)]
                )
                back[c, g, pl.ds(q * ORB, 8 * ORB)] = swap_blocks(tile).reshape(8 * ORB, LANES)

        home = rows_of(c * peers + me)
        pltpu.make_async_copy(
            back.at[c, gy, pl.ds(gx * piece, piece)], gathered.at[home], back_local.at[c]
        ).start()

        def one(k, carry):
            other, where = peer(k)
            pltpu.make_async_remote_copy(
                src_ref=back.at[c, lax.rem(other, ngy), pl.ds((other // ngy) * piece, piece)],
                dst_ref=gathered.at[home], send_sem=back_send.at[c], recv_sem=back_recv.at[c],
                device_id=where, device_id_type=MESH,
            ).start()
            return carry

        return lax.fori_loop(1, peers, one, carry)

    lax.fori_loop(0, chunks, one_chunk, 0)

    def wait_back(c, carry):
        pltpu.make_async_copy(
            block_ref.at[pl.ds(0, others)], gathered.at[pl.ds(0, others)], back_recv.at[c]
        ).wait()
        pltpu.make_async_copy(
            block_ref.at[pl.ds(0, piece)], gathered.at[pl.ds(0, piece)], back_local.at[c]
        ).wait()
        return carry

    lax.fori_loop(0, chunks, wait_back, 0)

    nvec = chunks * peers
    total = jnp.zeros((2 * nvec, nvec), jnp.float32)

    def gram_step(q, total):
        a = gathered[pl.ds(2 * q, nvec, stride=piece), :]
        b = gathered[pl.ds(2 * q + 1, nvec, stride=piece), :]
        high, low = split_bf16(jnp.concatenate([a, b], axis=1))
        return total + lax.dot_general(
            jnp.concatenate([high, low], axis=0), high, (((1,), (1,)), ((), ())),
            preferred_element_type=jnp.float32,
        )

    total = lax.fori_loop(0, piece // 2, gram_step, total)
    cross = total[nvec:]
    local = total[:nvec] + cross + cross.T
    grams[spot] = jnp.concatenate([local[: nvec // 2], local[nvec // 2:]], axis=1)
    share(plane, across, grams.at[spot], 2)
    out_copy = pltpu.make_async_copy(gathered, out_ref, out_sem)
    out_copy.start()
    settle(grams.at[pl.ds(0, plane - 1)], small_recv, 2)
    total = grams[0]
    for d in range(1, plane):
        total = total + grams[d]
    sums[z] = total
    share(nz, along, sums.at[z], 3)
    settle(sums.at[pl.ds(0, nz - 1)], small_recv, 3)
    total = sums[0]
    for d in range(1, nz):
        total = total + sums[d]
    gram_ref[...] = total

    def drain(c, carry):
        pltpu.make_async_copy(
            block_ref.at[pl.ds(0, others)], gathered.at[pl.ds(0, others)], send_sems.at[c]
        ).wait()
        return carry

    lax.fori_loop(0, chunks, drain, 0)

    def drain_back(c, carry):
        pltpu.make_async_copy(
            block_ref.at[pl.ds(0, others)], gathered.at[pl.ds(0, others)], back_send.at[c]
        ).wait()
        return carry

    lax.fori_loop(0, chunks, drain_back, 0)
    settle(columns.at[0, pl.ds(0, (nz - 1) * piece)], small_send, 0)
    settle(columns.at[pl.ds(0, plane - 1)], small_send, 1)
    settle(grams.at[pl.ds(0, plane - 1)], small_send, 2)
    settle(sums.at[pl.ds(0, nz - 1)], small_send, 3)
    out_copy.wait()


def basis_kernel(count, rows_ref, gram_ref, out_ref):
    nvec = gram_ref.shape[0] * 2
    piece = rows_ref.shape[0] // nvec
    packed = gram_ref[...] / count
    gram = jnp.concatenate([packed[:, :nvec], packed[:, nvec:]], axis=0)
    row = lax.broadcasted_iota(jnp.int32, (nvec, nvec), 0)
    lane = lax.broadcasted_iota(jnp.int32, (nvec, nvec), 1)
    work = jnp.concatenate([gram, (row == lane).astype(jnp.float32)], axis=1)
    full = (nvec, 2 * nvec)
    row = lax.broadcasted_iota(jnp.int32, full, 0)
    pivots = jnp.ones(full, jnp.float32)
    panel = 8
    for first in range(0, nvec, panel):
        cols = [
            jnp.broadcast_to(work[:, first + j:first + j + 1], full) for j in range(panel)
        ]
        for j in range(panel):
            k = first + j
            pivot = cols[j][k:k + 1]
            factor = jnp.where(row > k, cols[j] * (1.0 / pivot), 0.0)
            pivots = jnp.where(row == k, pivot, pivots)
            work = work - factor * work[k:k + 1]
            for i in range(j + 1, panel):
                cols[i] = cols[i] - factor * cols[i][k:k + 1]
    inverse = (work / jnp.sqrt(pivots))[:, nvec:]
    high, low = split_bf16(inverse)
    both = jnp.concatenate([high, low], axis=0)

    def one(q, carry):
        a = rows_ref[pl.ds(2 * q, nvec, stride=piece), :]
        b = rows_ref[pl.ds(2 * q + 1, nvec, stride=piece), :]
        vh, vl = split_bf16(jnp.concatenate([a, b], axis=1))
        twice = jnp.dot(both, vh, preferred_element_type=jnp.float32)
        out = twice[:nvec] + (twice[nvec:] + jnp.dot(high, vl, preferred_element_type=jnp.float32))
        out_ref[pl.ds(2 * q, nvec, stride=piece), :] = out[:, :LANES]
        out_ref[pl.ds(2 * q + 1, nvec, stride=piece), :] = out[:, LANES:]
        return carry

    lax.fori_loop(0, piece // 2, one, 0)


def per_device_whole(block, hop, onsite, offsets):
    ngx, ngy = lax.axis_size("gx"), lax.axis_size("gy")
    peers = ngx * ngy
    nvec, _, lx, ly = block.shape
    chunks = nvec // peers
    nx = ngx * lx
    piece = lx * ORB
    side = 2 * REACH + 1
    wide = spread_stencil(build_stencil(hop, offsets)).reshape(side, side, ORB, LANES)
    rows = jnp.transpose(block, (0, 2, 1, 3)).reshape(nvec * piece, ly)
    energy_rows = jnp.transpose(onsite, (1, 0, 2)).reshape(piece, ly)
    vmem = pl.BlockSpec(memory_space=pltpu.VMEM)
    hbm = pl.BlockSpec(memory_space=pl.ANY)
    filtered, packed = pl.pallas_call(
        functools.partial(filter_kernel, (ngx, ngy, chunks, lx)),
        out_shape=(
            jax.ShapeDtypeStruct((nvec * piece, ly), jnp.float32),
            jax.ShapeDtypeStruct((nvec // 2, LANES), jnp.float32),
        ),
        in_specs=[hbm, vmem, vmem],
        out_specs=(hbm, vmem),
        scratch_shapes=[
            pltpu.VMEM((side + 1, 2 * LANES, 2 * LANES), jnp.bfloat16),
            pltpu.VMEM((side + 1, 2 * LANES, 2 * LANES), jnp.bfloat16),
            pltpu.VMEM((chunks, ngy, nx * ORB, LANES), jnp.float32),
            pltpu.VMEM((2 * ngy, ngx // 2 * piece, LANES), jnp.float32),
            pltpu.VMEM((2, nx // 2, TY, LANES), jnp.float32),
            pltpu.VMEM((2, 2, nx // 2, TY, LANES), jnp.float32),
            pltpu.VMEM((2, nx // 2 + REACH, TY, 2 * LANES), jnp.bfloat16),
            pltpu.VMEM((2, nx // 2 + REACH, TY, 2 * LANES), jnp.bfloat16),
            pltpu.VMEM((chunks, ngy, nx * ORB, LANES), jnp.float32),
            pltpu.VMEM((nvec * piece, LANES), jnp.float32),
            pltpu.VMEM((2 * ngy, nvec // 2, LANES), jnp.float32),
            pltpu.VMEM((ngx // 2, nvec // 2, LANES), jnp.float32),
            pltpu.SemaphoreType.DMA((chunks,)),
            pltpu.SemaphoreType.DMA((chunks,)),
            pltpu.SemaphoreType.DMA((chunks,)),
            pltpu.SemaphoreType.DMA((chunks,)),
            pltpu.SemaphoreType.DMA((chunks,)),
            pltpu.SemaphoreType.DMA((chunks,)),
            pltpu.SemaphoreType.DMA((4,)),
            pltpu.SemaphoreType.DMA((4,)),
            pltpu.SemaphoreType.DMA,
        ],
        compiler_params=pltpu.CompilerParams(
            collective_id=0, has_side_effects=True, vmem_limit_bytes=48 * 1024 * 1024
        ),
    )(rows, energy_rows, wide)
    basis = pl.pallas_call(
        functools.partial(basis_kernel, piece * ly * peers),
        out_shape=jax.ShapeDtypeStruct((nvec * piece, ly), jnp.float32),
        in_specs=[vmem, vmem],
        out_specs=vmem,
        compiler_params=pltpu.CompilerParams(vmem_limit_bytes=32 * 1024 * 1024),
    )(filtered, packed)
    return jnp.transpose(basis.reshape(nvec, lx, ORB, ly), (0, 2, 1, 3))


def per_device(block, hop, onsite, offsets):
    ngx, ngy = lax.axis_size("gx"), lax.axis_size("gy")
    nvec, orbitals, lx, ly = block.shape
    fits = (
        nvec % (ngx * ngy) == 0 and nvec == 64 and orbitals == ORB and ly == LANES
        and ngy == 2 and ngx % 2 == 0 and ngx > 2 and (ngx * lx) % 16 == 0 and lx % 2 == 0
    )
    return (per_device_whole if fits else per_device_halo)(block, hop, onsite, offsets)


def solution(mesh):
    return jax.shard_map(
        per_device,
        mesh=mesh,
        in_specs=(
            P(None, None, ("grp", "gx"), "gy"),
            P("grp", None, None),
            P(None, ("grp", "gx"), "gy"),
            P(),
        ),
        out_specs=P(None, None, ("grp", "gx"), "gy"),
        check_vma=False,
    )
```

```python
import functools

import jax
import jax.numpy as jnp
from jax import lax
from jax.experimental import pallas as pl
from jax.experimental.pallas import tpu as pltpu
from jax.sharding import PartitionSpec as P

ORB = 8
REACH = 3
DEGREE = 4
NB = 49


shift_centre = 1.25
half_width = 2.25


def padded_2(array, sides, width):
    for axis, dim in sides:
        peers, length = (lax.axis_size(axis), array.shape[dim])
        up = [(i, (i + 1) % peers) for i in range(peers)]
        down = [(j, i) for i, j in up]
        last = lax.slice_in_dim(array, length - width, length, axis=dim)
        first = lax.slice_in_dim(array, 0, width, axis=dim)
        before = lax.ppermute(last, axis, up)
        after = lax.ppermute(first, axis, down)
        array = jnp.concatenate([before, array, after], axis=dim)
    return array


def build_stencil(hop, offsets):
    side = 2 * REACH + 1
    position = (offsets[:, 0] + REACH) * side + (offsets[:, 1] + REACH)
    slots = jnp.arange(NB, dtype=jnp.int32)
    onehot = (position[:, None] == slots[None, :]).astype(jnp.float32)
    flat = jnp.dot(
        onehot.T,
        hop.reshape(NB, ORB * ORB),
        precision=lax.Precision.HIGHEST,
        preferred_element_type=jnp.float32,
    )
    raw = jnp.transpose(flat.reshape(side, side, ORB, ORB), (2, 3, 0, 1))
    mirror = jnp.transpose(raw, (1, 0, 2, 3))[:, :, ::-1, ::-1]
    return 0.5 * (raw + mirror)


def hopping(padded, stencil):
    return lax.conv_general_dilated(
        padded,
        stencil,
        (1, 1),
        "VALID",
        dimension_numbers=("NCHW", "OIHW", "NCHW"),
        precision=lax.Precision.HIGHEST,
        preferred_element_type=jnp.float32,
    )


def extend(field, width):
    return padded_2(field, (("gx", 2), ("gy", 3)), width)


def advance(hopped, current, energies, previous):
    return (
        2.0 * (hopped + energies[None] * current - shift_centre * current) / half_width - previous
    )


def per_device_halo(block, hop, onsite, offsets):
    stencil = build_stencil(hop, offsets)
    vectors = block.shape[0]
    first_hop = hopping(extend(block, REACH), stencil)
    current = (first_hop + onsite[None] * block - shift_centre * block) / half_width
    previous = block
    for step in range(DEGREE - 1):
        following = advance(hopping(extend(current, REACH), stencil), current, onsite, previous)
        previous, current = (current, following)
    local_rows = current.shape[1] * current.shape[2] * current.shape[3]
    flat = current.reshape(vectors, local_rows)
    local_gram = jnp.dot(
        flat, flat.T, precision=lax.Precision.HIGHEST, preferred_element_type=jnp.float32
    )
    total_rows = local_rows * lax.axis_size("gx") * lax.axis_size("gy")
    gram = lax.psum(local_gram, ("gx", "gy")) / total_rows
    lower = jnp.linalg.cholesky(gram)
    inverse = lax.linalg.triangular_solve(
        lower, jnp.eye(vectors, dtype=jnp.float32), left_side=True, lower=True
    )
    basis = jnp.dot(
        inverse, flat, precision=lax.Precision.HIGHEST, preferred_element_type=jnp.float32
    )
    return basis.reshape(current.shape)


LANES = 128
TY = 16
MESH = pl.DeviceIdType.MESH


def split_bf16(value):
    high = value.astype(jnp.bfloat16)
    low = (value - high.astype(jnp.float32)).astype(jnp.bfloat16)
    return high, low


def spread_stencil(stencil):
    side = 2 * REACH + 1
    t = jnp.transpose(stencil, (2, 3, 1, 0)).reshape(side * side * ORB, ORB)
    lane = jnp.arange(LANES)
    spread = (lane[None, :] // TY == jnp.arange(ORB)[:, None]).astype(jnp.float32)
    return jnp.dot(t, spread, precision=lax.Precision.HIGHEST, preferred_element_type=jnp.float32)


def band_weights(wide_ref, wh_ref, wl_ref):
    side = 2 * REACH + 1
    yy = lax.broadcasted_iota(jnp.int32, (TY, LANES), 0)
    y = lax.rem(lax.broadcasted_iota(jnp.int32, (TY, LANES), 1), TY)
    empty = jnp.zeros((2 * LANES, LANES), jnp.bfloat16)
    for ref in (wh_ref, wl_ref):
        ref[0, :, pl.ds(LANES, LANES)] = empty
        ref[side, :, pl.ds(0, LANES)] = empty

    def one(dx, carry):
        for part in range(2):
            rel = yy if part == 0 else jnp.where(yy < TY // 2, yy + TY, yy - TY)
            dy = rel - y
            for p in range(ORB):
                total = jnp.zeros((TY, LANES), jnp.float32)
                for k in range(side):
                    row = wide_ref[dx, k, pl.ds(p, 1), :]
                    total = jnp.where(dy == k - REACH, row, total)
                high, low = split_bf16(total)
                rows = pl.ds(part * LANES + p * TY, TY)
                for xr in range(2):
                    wh_ref[dx + xr, rows, pl.ds(xr * LANES, LANES)] = high
                    wl_ref[dx + xr, rows, pl.ds(xr * LANES, LANES)] = low
        return carry

    lax.fori_loop(0, side, one, 0)


def swap_blocks(value):
    row = lax.broadcasted_iota(jnp.int32, value.shape, 1)
    blk = lax.broadcasted_iota(jnp.int32, value.shape, 2) // TY
    for bit in (1, 2, 4):
        a = (row // bit) % 2
        b = (blk // bit) % 2
        up = pltpu.roll(pltpu.roll(value, 8 - bit, 1), TY * bit, 2)
        down = up if bit == 4 else pltpu.roll(pltpu.roll(value, bit, 1), LANES - TY * bit, 2)
        value = jnp.where(a == b, value, jnp.where(a < b, up, down))
    return value


def filter_kernel(
    sizes, block_ref, onsite_ref, wide_ref, out_ref, gram_ref,
    wh_ref, wl_ref, recv, columns, energies, state, sh, sl, back, gathered, grams, sums,
    send_sems, recv_sems, local_sems, back_send, back_recv, back_local, small_send, small_recv, out_sem,
):
    ngx, ngy, chunks, lx = sizes
    peers = ngx * ngy
    nx = ngx * lx
    half = nx // 2
    piece = lx * ORB
    gx, gy = lax.axis_index("gx"), lax.axis_index("gy")
    me = gx * ngy + gy

    def peer(k):
        other = lax.rem(me + k, peers)
        return other, {"gx": other // ngy, "gy": lax.rem(other, ngy)}

    barrier = pltpu.get_barrier_semaphore()

    def greet(k, carry):
        pl.semaphore_signal(barrier, inc=1, device_id=peer(k)[1], device_id_type=MESH)
        return carry

    lax.fori_loop(1, peers, greet, 0)
    pl.semaphore_wait(barrier, peers - 1)

    def rows_of(vector):
        return pl.ds(vector * piece, piece)

    def landing(c):
        return recv.at[c, gy, pl.ds(gx * piece, piece)]

    plane = 2 * ngy
    nz = ngx // 2
    z, col = gx // 2, lax.rem(gx, 2)
    spot = col * ngy + gy

    def along(k):
        return {"gx": lax.rem(z + k, nz) * 2 + col, "gy": gy}

    def across(k):
        other = lax.rem(spot + k, plane)
        return {"gx": z * 2 + other // ngy, "gy": lax.rem(other, ngy)}

    def share(count, where, ref, sem):
        def one(k, carry):
            pltpu.make_async_remote_copy(
                src_ref=ref, dst_ref=ref, send_sem=small_send.at[sem],
                recv_sem=small_recv.at[sem], device_id=where(k), device_id_type=MESH,
            ).start()
            return carry

        lax.fori_loop(1, count, one, 0)

    def settle(refs, sems, sem):
        pltpu.make_async_copy(refs, refs, sems.at[sem]).wait()

    columns[spot, pl.ds(z * piece, piece)] = onsite_ref[...]
    share(nz, along, columns.at[spot, pl.ds(z * piece, piece)], 0)

    def send_chunk(c, carry):
        pltpu.make_async_copy(
            block_ref.at[rows_of(c * peers + me)], landing(c), local_sems.at[c]
        ).start()

        def one(k, carry):
            other, where = peer(k)
            pltpu.make_async_remote_copy(
                src_ref=block_ref.at[rows_of(c * peers + other)], dst_ref=landing(c),
                send_sem=send_sems.at[c], recv_sem=recv_sems.at[c],
                device_id=where, device_id_type=MESH,
            ).start()
            return carry

        return lax.fori_loop(1, peers, one, carry)

    send_chunk(0, 0)
    settle(columns.at[0, pl.ds(0, (nz - 1) * piece)], small_recv, 0)
    share(plane, across, columns.at[spot], 1)
    lax.fori_loop(1, chunks, send_chunk, 0)
    band_weights(wide_ref, wh_ref, wl_ref)

    others = (peers - 1) * piece

    def wait_chunk(c):
        pltpu.make_async_copy(
            block_ref.at[pl.ds(0, others)], gathered.at[pl.ds(0, others)], recv_sems.at[c]
        ).wait()
        pltpu.make_async_copy(block_ref.at[pl.ds(0, piece)], landing(c), local_sems.at[c]).wait()

    def unpack(c, store):
        for g in range(ngy):
            for q in range(0, nx, 8):
                tile = recv[c, g, pl.ds(q * ORB, 8 * ORB)].reshape(8, ORB, LANES)
                tile = swap_blocks(tile)
                for i in range(8):
                    x = q + i
                    store(x % 2, x // 2, g, tile[i])

    settle(columns.at[pl.ds(0, plane - 1)], small_recv, 1)
    for other in range(plane):
        for q in range(nz):
            tile = columns[other, pl.ds(q * piece, piece)].reshape(lx, ORB, LANES)
            tile = swap_blocks(tile) - shift_centre
            for i in range(lx):
                x = (2 * q + other // ngy) * lx + i
                energies[x % 2, x // 2, pl.ds((other % ngy) * 8, 8), :] = tile[i]

    lane = lax.broadcasted_iota(jnp.int32, (1, TY, LANES), 2)
    near = lax.rem(lane, TY) < TY // 2
    low_rows = {1: (1, [(0, half - 1), (half + 1, 0), (half + 2, 1)]),
                0: (2, [(0, half - 2), (1, half - 1), (half + 2, 0)])}

    def one_chunk(c, carry):
        wait_chunk(c)

        def store_state(xr, r, g, tile):
            state[0, xr, r, pl.ds(g * 8, 8), :] = tile
            state[1, xr, r, pl.ds(g * 8, 8), :] = jnp.zeros_like(tile)

        unpack(c, store_state)

        def step(k, carry):
            now = lax.rem(k, 2)
            for xr in range(2):
                par = 1 - xr
                start, wraps = low_rows[par]
                for r in range(0, half, 4):
                    v = state[now, xr, pl.ds(r, 4)]
                    edge = jnp.where(near, pltpu.roll(v, TY - 1, 1), pltpu.roll(v, 1, 1))
                    both = jnp.concatenate([v, edge], axis=2)
                    high, low = split_bf16(both)
                    sh[par, pl.ds(start + r, 4)] = high
                    sl[par, pl.ds(start + r, 4)] = low
                for to, r in wraps:
                    sh[par, to] = sh[par, start + r]
                    sl[par, to] = sl[par, start + r]
            alpha = jnp.where(k == 0, 1.0 / half_width, 2.0 / half_width)
            for r in range(0, half, 8):
                acc = jnp.zeros((8 * TY, 2 * LANES), jnp.float32)
                for j in range(2 * REACH + 2):
                    rows = pl.ds(r + j // 2, 8)
                    vh = sh[j % 2, rows].reshape(8 * TY, 2 * LANES)
                    vl = sl[j % 2, rows].reshape(8 * TY, 2 * LANES)
                    acc += jnp.dot(vh, wh_ref[j], preferred_element_type=jnp.float32)
                    acc += jnp.dot(vl, wh_ref[j], preferred_element_type=jnp.float32)
                    acc += jnp.dot(vh, wl_ref[j], preferred_element_type=jnp.float32)
                for xr in range(2):
                    hopped = acc[:, xr * LANES:(xr + 1) * LANES].reshape(8, TY, LANES)
                    v = state[now, xr, pl.ds(r, 8)]
                    e = energies[xr, pl.ds(r, 8)]
                    old = state[1 - now, xr, pl.ds(r, 8)]
                    state[1 - now, xr, pl.ds(r, 8)] = alpha * (hopped + e * v) - old
            return carry

        lax.fori_loop(0, DEGREE, step, 0)

        for g in range(ngy):
            for q in range(0, nx, 8):
                tile = jnp.stack(
                    [state[DEGREE % 2, (q + i) % 2, (q + i) // 2, pl.ds(g * 8, 8), :] for i in range(8)]
                )
                back[c, g, pl.ds(q * ORB, 8 * ORB)] = swap_blocks(tile).reshape(8 * ORB, LANES)

        home = rows_of(c * peers + me)
        pltpu.make_async_copy(
            back.at[c, gy, pl.ds(gx * piece, piece)], gathered.at[home], back_local.at[c]
        ).start()

        def one(k, carry):
            other, where = peer(k)
            pltpu.make_async_remote_copy(
                src_ref=back.at[c, lax.rem(other, ngy), pl.ds((other // ngy) * piece, piece)],
                dst_ref=gathered.at[home], send_sem=back_send.at[c], recv_sem=back_recv.at[c],
                device_id=where, device_id_type=MESH,
            ).start()
            return carry

        return lax.fori_loop(1, peers, one, carry)

    lax.fori_loop(0, chunks, one_chunk, 0)

    def wait_back(c, carry):
        pltpu.make_async_copy(
            block_ref.at[pl.ds(0, others)], gathered.at[pl.ds(0, others)], back_recv.at[c]
        ).wait()
        pltpu.make_async_copy(
            block_ref.at[pl.ds(0, piece)], gathered.at[pl.ds(0, piece)], back_local.at[c]
        ).wait()
        return carry

    lax.fori_loop(0, chunks, wait_back, 0)

    nvec = chunks * peers
    total = jnp.zeros((2 * nvec, nvec), jnp.float32)

    def gram_step(q, total):
        a = gathered[pl.ds(2 * q, nvec, stride=piece), :]
        b = gathered[pl.ds(2 * q + 1, nvec, stride=piece), :]
        high, low = split_bf16(jnp.concatenate([a, b], axis=1))
        return total + lax.dot_general(
            jnp.concatenate([high, low], axis=0), high, (((1,), (1,)), ((), ())),
            preferred_element_type=jnp.float32,
        )

    total = lax.fori_loop(0, piece // 2, gram_step, total, unroll=8)
    cross = total[nvec:]
    local = total[:nvec] + cross + cross.T
    grams[spot] = jnp.concatenate([local[: nvec // 2], local[nvec // 2:]], axis=1)
    share(plane, across, grams.at[spot], 2)
    out_copy = pltpu.make_async_copy(gathered, out_ref, out_sem)
    out_copy.start()
    settle(grams.at[pl.ds(0, plane - 1)], small_recv, 2)
    total = grams[0]
    for d in range(1, plane):
        total = total + grams[d]
    sums[z] = total
    share(nz, along, sums.at[z], 3)
    settle(sums.at[pl.ds(0, nz - 1)], small_recv, 3)
    total = sums[0]
    for d in range(1, nz):
        total = total + sums[d]
    gram_ref[...] = total

    def drain(c, carry):
        pltpu.make_async_copy(
            block_ref.at[pl.ds(0, others)], gathered.at[pl.ds(0, others)], send_sems.at[c]
        ).wait()
        return carry

    lax.fori_loop(0, chunks, drain, 0)

    def drain_back(c, carry):
        pltpu.make_async_copy(
            block_ref.at[pl.ds(0, others)], gathered.at[pl.ds(0, others)], back_send.at[c]
        ).wait()
        return carry

    lax.fori_loop(0, chunks, drain_back, 0)
    settle(columns.at[0, pl.ds(0, (nz - 1) * piece)], small_send, 0)
    settle(columns.at[pl.ds(0, plane - 1)], small_send, 1)
    settle(grams.at[pl.ds(0, plane - 1)], small_send, 2)
    settle(sums.at[pl.ds(0, nz - 1)], small_send, 3)
    out_copy.wait()


def basis_kernel(count, rows_ref, gram_ref, out_ref):
    nvec = gram_ref.shape[0] * 2
    piece = rows_ref.shape[0] // nvec
    packed = gram_ref[...] / count
    gram = jnp.concatenate([packed[:, :nvec], packed[:, nvec:]], axis=0)
    row = lax.broadcasted_iota(jnp.int32, (nvec, nvec), 0)
    lane = lax.broadcasted_iota(jnp.int32, (nvec, nvec), 1)
    work = jnp.concatenate([gram, (row == lane).astype(jnp.float32)], axis=1)
    full = (nvec, 2 * nvec)
    row = lax.broadcasted_iota(jnp.int32, full, 0)
    pivots = jnp.ones(full, jnp.float32)
    panel = 8
    for first in range(0, nvec, panel):
        cols = [
            jnp.broadcast_to(work[:, first + j:first + j + 1], full) for j in range(panel)
        ]
        for j in range(panel):
            k = first + j
            pivot = cols[j][k:k + 1]
            factor = jnp.where(row > k, cols[j] * (1.0 / pivot), 0.0)
            pivots = jnp.where(row == k, pivot, pivots)
            work = work - factor * work[k:k + 1]
            for i in range(j + 1, panel):
                cols[i] = cols[i] - factor * cols[i][k:k + 1]
    inverse = (work / jnp.sqrt(pivots))[:, nvec:]
    high, low = split_bf16(inverse)
    both = jnp.concatenate([high, low], axis=0)

    def one(q, carry):
        a = rows_ref[pl.ds(2 * q, nvec, stride=piece), :]
        b = rows_ref[pl.ds(2 * q + 1, nvec, stride=piece), :]
        vh, vl = split_bf16(jnp.concatenate([a, b], axis=1))
        twice = jnp.dot(both, vh, preferred_element_type=jnp.float32)
        out = twice[:nvec] + (twice[nvec:] + jnp.dot(high, vl, preferred_element_type=jnp.float32))
        out_ref[pl.ds(2 * q, nvec, stride=piece), :] = out[:, :LANES]
        out_ref[pl.ds(2 * q + 1, nvec, stride=piece), :] = out[:, LANES:]
        return carry

    lax.fori_loop(0, piece // 2, one, 0, unroll=4)


def per_device_whole(block, hop, onsite, offsets):
    ngx, ngy = lax.axis_size("gx"), lax.axis_size("gy")
    peers = ngx * ngy
    nvec, _, lx, ly = block.shape
    chunks = nvec // peers
    nx = ngx * lx
    piece = lx * ORB
    side = 2 * REACH + 1
    wide = spread_stencil(build_stencil(hop, offsets)).reshape(side, side, ORB, LANES)
    rows = jnp.transpose(block, (0, 2, 1, 3)).reshape(nvec * piece, ly)
    energy_rows = jnp.transpose(onsite, (1, 0, 2)).reshape(piece, ly)
    vmem = pl.BlockSpec(memory_space=pltpu.VMEM)
    hbm = pl.BlockSpec(memory_space=pl.ANY)
    filtered, packed = pl.pallas_call(
        functools.partial(filter_kernel, (ngx, ngy, chunks, lx)),
        out_shape=(
            jax.ShapeDtypeStruct((nvec * piece, ly), jnp.float32),
            jax.ShapeDtypeStruct((nvec // 2, LANES), jnp.float32),
        ),
        in_specs=[hbm, vmem, vmem],
        out_specs=(hbm, vmem),
        scratch_shapes=[
            pltpu.VMEM((side + 1, 2 * LANES, 2 * LANES), jnp.bfloat16),
            pltpu.VMEM((side + 1, 2 * LANES, 2 * LANES), jnp.bfloat16),
            pltpu.VMEM((chunks, ngy, nx * ORB, LANES), jnp.float32),
            pltpu.VMEM((2 * ngy, ngx // 2 * piece, LANES), jnp.float32),
            pltpu.VMEM((2, nx // 2, TY, LANES), jnp.float32),
            pltpu.VMEM((2, 2, nx // 2, TY, LANES), jnp.float32),
            pltpu.VMEM((2, nx // 2 + REACH, TY, 2 * LANES), jnp.bfloat16),
            pltpu.VMEM((2, nx // 2 + REACH, TY, 2 * LANES), jnp.bfloat16),
            pltpu.VMEM((chunks, ngy, nx * ORB, LANES), jnp.float32),
            pltpu.VMEM((nvec * piece, LANES), jnp.float32),
            pltpu.VMEM((2 * ngy, nvec // 2, LANES), jnp.float32),
            pltpu.VMEM((ngx // 2, nvec // 2, LANES), jnp.float32),
            pltpu.SemaphoreType.DMA((chunks,)),
            pltpu.SemaphoreType.DMA((chunks,)),
            pltpu.SemaphoreType.DMA((chunks,)),
            pltpu.SemaphoreType.DMA((chunks,)),
            pltpu.SemaphoreType.DMA((chunks,)),
            pltpu.SemaphoreType.DMA((chunks,)),
            pltpu.SemaphoreType.DMA((4,)),
            pltpu.SemaphoreType.DMA((4,)),
            pltpu.SemaphoreType.DMA,
        ],
        compiler_params=pltpu.CompilerParams(
            collective_id=0, has_side_effects=True, vmem_limit_bytes=48 * 1024 * 1024
        ),
    )(rows, energy_rows, wide)
    basis = pl.pallas_call(
        functools.partial(basis_kernel, piece * ly * peers),
        out_shape=jax.ShapeDtypeStruct((nvec * piece, ly), jnp.float32),
        in_specs=[vmem, vmem],
        out_specs=vmem,
        compiler_params=pltpu.CompilerParams(vmem_limit_bytes=32 * 1024 * 1024),
    )(filtered, packed)
    return jnp.transpose(basis.reshape(nvec, lx, ORB, ly), (0, 2, 1, 3))


def per_device(block, hop, onsite, offsets):
    ngx, ngy = lax.axis_size("gx"), lax.axis_size("gy")
    nvec, orbitals, lx, ly = block.shape
    fits = (
        nvec % (ngx * ngy) == 0 and nvec == 64 and orbitals == ORB and ly == LANES
        and ngy == 2 and ngx % 2 == 0 and ngx > 2 and (ngx * lx) % 16 == 0 and lx % 2 == 0
    )
    return (per_device_whole if fits else per_device_halo)(block, hop, onsite, offsets)


def solution(mesh):
    return jax.shard_map(
        per_device,
        mesh=mesh,
        in_specs=(
            P(None, None, ("grp", "gx"), "gy"),
            P("grp", None, None),
            P(None, ("grp", "gx"), "gy"),
            P(),
        ),
        out_specs=P(None, None, ("grp", "gx"), "gy"),
        check_vma=False,
    )
```
